1024 devices in a mesh: tower: 8 (over x, core), inner: 128 (over z, y).
Axes of the slice: x: 4, y: 4, z: 32, core: 2. Of those that a mesh axis runs over, the one named last changes fastest.
Arguments:
- grad_inter: bfloat16 [128, 16, 8192], P('inner', 'tower'), may hold values from -6 to 6
- pooled: bfloat16 [8, 2048, 16384], P('tower', None, 'inner'), may hold values from -6 to 6
- tower_weight: bfloat16 [8, 16384, 1024], P('tower', 'inner'), may hold values from -0.1875 to 0.1875
- indices: int32 [8, 128, 2048, 16], P('tower', 'inner'), may hold values from 0 to 1023
- lengths: int32 [8, 128, 2048], P('tower', 'inner'), may hold values from 1 to 16, as said below
- table_slab: float32 [8, 131072, 128], P('tower', 'inner'), may hold values from -0.3 to 0.3
- accumulator: float32 [8, 131072, 128], P('tower', 'inner'), may hold values from 0.1 to 1
Outputs:
- weight_grad: float32 [8, 16384, 1024], P('tower', 'inner')
- new_table: float32 [8, 131072, 128], P('tower', 'inner')
- new_accum: float32 [8, 131072, 128], P('tower', 'inner')
The draws below stay inside these ranges and needn't reach their ends.
Inputs may be any that keep to these rules, and one draw needn't show every extreme that they name: Only the first lengths entries of a bag are live; every device holds some bag of length 16.
All inputs are finite; a program needn't handle non-finite values.
Results may differ from the reference program's by a relative error of at most 0.0051.
Values may be sent and summed in bfloat16 or wider, within the bound.
No kernel may reach another device: no remote copies, remote signals or barrier semaphores. Data moves between devices by JAX's collectives and lax.ppermute only.
A program may use at most 32 MiB of HBM per device.

```python
import math
import jax
import jax.numpy as jnp
from jax import lax

CW = 1024
EMB = 128
BAG = 16
ROWS = 1024
S_DEV = 2
TOWERS = 8
FEATS = 128
TOWER_IN = 16384
SAMPLES = 2048


def draw_lengths(key, part):
    key = jax.random.fold_in(key, 7)
    values = jax.random.randint(key, (TOWERS, FEATS, SAMPLES), 1, BAG + 1, dtype=jnp.int32)
    return values.at[:, :, 0].set(BAG)


def set_ends(drawn, key, smallest, high):
    extent = drawn.shape
    spot = [jax.random.randint(jax.random.fold_in(key, axis), (), 0, extent[axis]) for axis in range(len(extent))]
    drawn = drawn.at[tuple(spot)].set(smallest)
    longest = extent.index(max(extent))
    spot[longest] = (spot[longest] + 1) % extent[longest]
    return drawn.at[tuple(spot)].set(high)


def shard_levels(own_key, dims, shards, smallest, high):
    def one(axis_at, blocks):
        heights = jax.random.uniform(jax.random.fold_in(jax.random.fold_in(own_key, 6), axis_at), (blocks,), jnp.float32, smallest / len(shards), high / len(shards))
        return jnp.repeat(jnp.exp(heights), dims[axis_at] // blocks).reshape((-1,) + (1,) * (len(dims) - axis_at - 1))

    gain = one(*shards[0])
    for cut in shards[1:]:
        gain = gain * one(*cut)
    return gain


def gaussian(rng, extent, spread, limit, shards=(), kind=jnp.bfloat16):
    result = jax.random.normal(rng, extent, jnp.float32) * spread
    if len(shards) > 0:
        result = shard_levels(rng, extent, shards, -0.22, 0.18) * result
    return jnp.clip(result, min=-limit, max=limit).astype(kind)


def setup_inputs(seed: int = 0) -> dict:
    key_list = jax.random.split(jax.random.key(seed), 8)
    grad_inter = gaussian(key_list[0], (FEATS, TOWERS * S_DEV, TOWERS * CW), 1.0, 6.0, ((0, 128), (1, 8)))
    pooled = gaussian(key_list[1], (TOWERS, SAMPLES, TOWER_IN), 1.0, 6.0, ((0, 8), (2, 128)))
    tower_weight = gaussian(key_list[2], (TOWERS, TOWER_IN, CW), CW ** -0.5, 0.1875, ((0, 8), (1, 128)))
    indices = set_ends(jax.random.randint(key_list[3], (TOWERS, FEATS, SAMPLES, BAG), 0, ROWS), jax.random.fold_in(key_list[3], 1), 0, ROWS - 1).astype(jnp.int32)
    lengths = draw_lengths(jax.random.fold_in(key_list[7], 71), 0)
    table_slab = gaussian(key_list[5], (TOWERS, FEATS * ROWS, EMB), 0.05, 0.3, ((0, 8), (1, 128)), jnp.float32)
    accumulator = jnp.clip(jnp.exp(math.log(1.0) - 2.3025851 * jax.random.uniform(key_list[6], (TOWERS, FEATS * ROWS, EMB), jnp.float32) ** shard_levels(key_list[6], (TOWERS, FEATS * ROWS, EMB), ((0, 8), (1, 128)), -0.2, 0.2)), 0.1, 1.0)
    return {"grad_inter": grad_inter, "pooled": pooled, "tower_weight": tower_weight, "indices": indices, "lengths": lengths, "table_slab": table_slab, "accumulator": accumulator}


learn_rate = 0.1
epsilon = 1e-08

def feature_grad(inputs):
    pool_cols, index_rows, bag_lengths = inputs
    live = (jnp.arange(BAG)[None, :] < bag_lengths[:, None]).astype(jnp.float32)
    values = pool_cols.astype(jnp.float32)[:, None, :] * live[:, :, None]
    zeros = jnp.zeros((ROWS, EMB), jnp.float32)
    return zeros.at[index_rows.reshape(-1)].add(values.reshape(-1, EMB))

def tower_step(inputs):
    cotangent, feats, weights, index_all, length_all, slab, sums = inputs
    wgrad = lax.dot_general(feats, cotangent, (((0,), (0,)), ((), ())), preferred_element_type=jnp.float32)
    pgrad = lax.dot_general(cotangent, weights, (((1,), (1,)), ((), ())), preferred_element_type=jnp.float32).astype(jnp.bfloat16)
    per_feature = pgrad.reshape(SAMPLES, FEATS, EMB).transpose(1, 0, 2)
    row_grad = lax.map(feature_grad, (per_feature, index_all, length_all)).reshape(FEATS * ROWS, EMB)
    fresh = sums + row_grad * row_grad
    updated = slab - learn_rate * row_grad / (jnp.sqrt(fresh) + epsilon)
    return (wgrad, updated, fresh)

def reference(grad_inter, pooled, tower_weight, indices, lengths, table_slab, accumulator):
    flat = grad_inter.reshape(SAMPLES, TOWERS, CW).transpose(1, 0, 2)
    return lax.map(tower_step, (flat, pooled, tower_weight, indices, lengths, table_slab, accumulator))
```

```python
import functools

import jax
import jax.numpy as jnp
from jax import lax
from jax.experimental import pallas as pl
from jax.experimental.pallas import tpu as pltpu
from jax.sharding import Mesh, PartitionSpec as P

learn_rate = 0.1
epsilon = 1e-08

Z_PARTS = (4, 4, 2)
RING = ("a", "b")
BLOCK = ("c", "y")
INNER = ("a", "b", "c", "y")

BF16 = jnp.bfloat16
F32 = jnp.float32


def split_kernel(x_ref, o_ref):
    towers, _, width = o_ref.shape
    for t in range(towers):
        o_ref[t] = x_ref[:, t * width:(t + 1) * width]


def split_towers(x, towers):
    rows, width = x.shape
    return pl.pallas_call(
        split_kernel,
        out_shape=jax.ShapeDtypeStruct((towers, rows, width // towers), x.dtype),
    )(x)


def count_kernel(index_ref, length_ref, o_ref):
    bag, _ = index_ref.shape
    rows, lanes = o_ref.shape
    step = 16
    bag_at = lax.broadcasted_iota(jnp.int32, index_ref.shape, 0)
    live = jnp.where(bag_at < length_ref[...], index_ref[...], -1)
    entries = [
        jnp.broadcast_to(live[b:b + 1, :], (step, lanes)).astype(jnp.int16) for b in range(bag)
    ]
    first = lax.broadcasted_iota(jnp.int32, (step, lanes), 0)

    def body(k, _):
        low = pl.multiple_of(k * step, step)
        row = (first + low).astype(jnp.int16)
        parts = [jnp.where(e == row, jnp.ones((), BF16), jnp.zeros((), BF16)) for e in entries]
        while len(parts) > 1:
            parts = [parts[i] + parts[i + 1] for i in range(0, len(parts), 2)]
        o_ref[pl.ds(low, step), :] = parts[0]
        return 0

    lax.fori_loop(0, rows // step, body, 0, unroll=4)


def bag_counts(index_cols, bag_lengths, rows):
    bag, samples = index_cols.shape
    lanes = 128
    return pl.pallas_call(
        count_kernel,
        grid=(samples // lanes,),
        in_specs=[
            pl.BlockSpec((bag, lanes), lambda i: (0, i)),
            pl.BlockSpec((1, lanes), lambda i: (0, i)),
        ],
        out_specs=pl.BlockSpec((rows, lanes), lambda i: (0, i)),
        out_shape=jax.ShapeDtypeStruct((rows, samples), BF16),
        cost_estimate=pl.CostEstimate(
            flops=3 * bag * rows * samples, bytes_accessed=2 * rows * samples, transcendentals=0
        ),
    )(index_cols, bag_lengths)


def update_kernel(
    chunks, cot_ref, pooled_ref, weight_ref, counts_ref, slab_ref, sums_ref,
    wgrad_ref, table_ref, fresh_ref, pgrad_ref,
):
    k = pl.program_id(0)

    @pl.when(k == 0)
    def _():
        wgrad_ref[...] = jnp.zeros_like(wgrad_ref)

    @pl.when(k < chunks)
    def _():
        cot = cot_ref[0]
        rows = cot.shape[0]
        emb = weight_ref.shape[0]
        feats = pooled_ref[:, k].reshape(rows, emb)
        wgrad_ref[...] += lax.dot_general(
            feats, cot, (((0,), (0,)), ((), ())), preferred_element_type=F32
        )
        pgrad = lax.dot_general(
            cot, weight_ref[...], (((1,), (1,)), ((), ())), preferred_element_type=F32
        ).astype(BF16)
        pgrad_ref[:, k] = pgrad.reshape(pgrad_ref.shape[0], pgrad_ref.shape[2], emb)

    @pl.when(k >= chunks)
    def _():
        rows, lanes = pgrad_ref.shape[0] * pgrad_ref.shape[1] * pgrad_ref.shape[2], pgrad_ref.shape[3]
        row_grad = jnp.dot(
            counts_ref[...], pgrad_ref[...].reshape(rows, lanes), preferred_element_type=F32
        )
        fresh = sums_ref[...] + row_grad * row_grad
        fresh_ref[...] = fresh
        table_ref[...] = slab_ref[...] - learn_rate * row_grad / (jnp.sqrt(fresh) + epsilon)


def update(gathered, own, feats, weights, counts, slab, sums):
    chunks, rows, width = gathered.shape
    samples, emb = feats.shape
    groups = rows // own
    feats = feats.reshape(groups, chunks, own, emb)
    slab_rows = slab.shape[0]
    steps = 4
    tile = slab_rows // steps
    first = lambda k: jnp.minimum(k, chunks - 1)
    second = lambda k: jnp.maximum(k - chunks, 0)
    return pl.pallas_call(
        functools.partial(update_kernel, chunks),
        grid=(chunks + steps,),
        in_specs=[
            pl.BlockSpec((1, rows, width), lambda k: (first(k), 0, 0)),
            pl.BlockSpec((groups, chunks, own, emb), lambda k: (0, 0, 0, 0)),
            pl.BlockSpec((emb, width), lambda k: (0, 0)),
            pl.BlockSpec((tile, samples), lambda k: (second(k), 0)),
            pl.BlockSpec((tile, emb), lambda k: (second(k), 0)),
            pl.BlockSpec((tile, emb), lambda k: (second(k), 0)),
        ],
        out_specs=[
            pl.BlockSpec((emb, width), lambda k: (0, 0)),
            pl.BlockSpec((tile, emb), lambda k: (second(k), 0)),
            pl.BlockSpec((tile, emb), lambda k: (second(k), 0)),
        ],
        out_shape=[
            jax.ShapeDtypeStruct((emb, width), F32),
            jax.ShapeDtypeStruct((slab_rows, emb), F32),
            jax.ShapeDtypeStruct((slab_rows, emb), F32),
        ],
        scratch_shapes=[pltpu.VMEM((groups, chunks, own, emb), BF16)],
        compiler_params=pltpu.CompilerParams(vmem_limit_bytes=32 * 1024 * 1024),
        cost_estimate=pl.CostEstimate(
            flops=4 * samples * emb * width + 2 * samples * emb * slab_rows,
            bytes_accessed=2 * samples * (width + slab_rows) + 16 * slab_rows * emb,
            transcendentals=slab_rows * emb,
        ),
    )(gathered, feats, weights, counts, slab, sums)


def per_device(grad_inter, pooled, tower_weight, indices, lengths, table_slab, accumulator):
    towers = lax.axis_size("tower")
    members = lax.axis_size(BLOCK)
    counts = bag_counts(indices[0, 0].T, lengths[0], table_slab.shape[1])
    parted = split_towers(grad_inter[0], towers)
    own = lax.all_to_all(parted, "tower", split_axis=0, concat_axis=0)
    own = own.reshape(-1, own.shape[2])
    ring = lax.all_gather(own, RING, axis=0, tiled=True)
    gathered = lax.all_to_all(
        jnp.broadcast_to(ring[None], (members,) + ring.shape), BLOCK, split_axis=0, concat_axis=0
    )
    wgrad, updated, fresh = update(
        gathered, own.shape[0], pooled[0], tower_weight[0], counts, table_slab[0], accumulator[0]
    )
    return (wgrad[None], updated[None], fresh[None])


def solution(mesh):
    towers, inner = mesh.devices.shape
    shape = (towers,) + Z_PARTS + (inner // (Z_PARTS[0] * Z_PARTS[1] * Z_PARTS[2]),)
    fine = Mesh(mesh.devices.reshape(shape), ("tower",) + INNER)
    return jax.shard_map(
        per_device,
        mesh=fine,
        in_specs=(
            P(INNER, "tower", None),
            P("tower", None, INNER),
            P("tower", INNER, None),
            P("tower", INNER, None, None),
            P("tower", INNER, None),
            P("tower", INNER, None),
            P("tower", INNER, None),
        ),
        out_specs=(P("tower", INNER, None), P("tower", INNER, None), P("tower", INNER, None)),
        check_vma=False,
    )
```

```python
import functools

import jax
import jax.numpy as jnp
from jax import lax
from jax.experimental import pallas as pl
from jax.experimental.pallas import tpu as pltpu
from jax.sharding import Mesh, PartitionSpec as P

learn_rate = 0.1
epsilon = 1e-08

HALVES = 2
RING, HALF, SIDE = "ring", "half", "side"
INNER = (RING, HALF, SIDE)
PAIRED = ("tower", RING, HALF)

BF16 = jnp.bfloat16
F32 = jnp.float32
LIMIT = pltpu.CompilerParams(vmem_limit_bytes=20 * 1024 * 1024)


def partners(towers, length):
    pairs = []
    for t in range(towers):
        for z in range(length):
            up = (z + t) % 2 == 0
            pairs.append((t * length + z, t * length + (z + (1 if up else -1)) % length))
    return pairs


def across(w):
    rows, cols = w.shape
    return jnp.concatenate([w[:, i:i + rows] for i in range(0, cols, rows)], axis=0)


def along(w, rows):
    return jnp.concatenate([w[i:i + rows] for i in range(0, w.shape[0], rows)], axis=1)


def prepare_kernel(half_ref, x_ref, pooled_ref, weight_ref, o_ref, send_ref):
    towers, _, width = o_ref.shape
    for t in range(towers):
        o_ref[t] = x_ref[:, t * width:(t + 1) * width]
    send_ref[0] = pooled_ref[:, 0]
    send_ref[1] = across(weight_ref[...]).reshape(send_ref.shape[1:])


def prepare(half, x, towers, feats, weights):
    rows, width = x.shape
    ring, halves, sides, own, emb = feats.shape
    return pl.pallas_call(
        prepare_kernel,
        grid_spec=pltpu.PrefetchScalarGridSpec(
            num_scalar_prefetch=1,
            grid=(1,),
            in_specs=[
                pl.BlockSpec(x.shape, lambda k, h: (0, 0)),
                pl.BlockSpec((ring, 1, sides, own, emb), lambda k, h: (0, 1 - h[0], 0, 0, 0)),
                pl.BlockSpec(weights.shape, lambda k, h: (0, 0)),
            ],
            out_specs=[
                pl.BlockSpec((towers, rows, width // towers), lambda k, h: (0, 0, 0)),
                pl.BlockSpec((2, ring, sides, own, emb), lambda k, h: (0, 0, 0, 0, 0)),
            ],
        ),
        out_shape=[
            jax.ShapeDtypeStruct((towers, rows, width // towers), BF16),
            jax.ShapeDtypeStruct((2, ring, sides, own, emb), BF16),
        ],
    )(half, x, feats, weights)


def count_kernel(half_ref, index_ref, length_ref, o_ref, done_ref):
    done_ref[...] = jnp.zeros_like(done_ref)
    bag, width = index_ref.shape
    _, rows, lanes = o_ref.shape
    step = 16
    run = lanes // 2
    bag_at = lax.broadcasted_iota(jnp.int32, index_ref.shape, 0)
    live = jnp.where(bag_at < length_ref[...], index_ref[...], -1)
    left, right = live[:, :lanes], live[:, lanes:]
    low_lane = lax.broadcasted_iota(jnp.int32, left.shape, 1) < run
    halves = [
        jnp.where(low_lane, left, pltpu.roll(right, run, 1)),
        jnp.where(low_lane, pltpu.roll(left, run, 1), right),
    ]
    upper = half_ref[0] == 1
    first = lax.broadcasted_iota(jnp.int32, (step, lanes), 0)
    for side in range(2):
        chosen = jnp.where(upper, halves[1 - side], halves[side])
        entries = [
            jnp.broadcast_to(chosen[b:b + 1, :], (step, lanes)).astype(jnp.int16)
            for b in range(bag)
        ]

        def body(k, _, entries=entries, side=side):
            low = pl.multiple_of(k * step, step)
            row = (first + low).astype(jnp.int16)
            parts = [jnp.where(e == row, jnp.ones((), BF16), jnp.zeros((), BF16)) for e in entries]
            while len(parts) > 1:
                parts = [parts[i] + parts[i + 1] for i in range(0, len(parts), 2)]
            o_ref[side, pl.ds(low, step), :] = parts[0]
            return 0

        lax.fori_loop(0, rows // step, body, 0, unroll=4)


def bag_counts(half, index_cols, bag_lengths, rows):
    bag, samples = index_cols.shape
    lanes = 128
    return pl.pallas_call(
        count_kernel,
        grid_spec=pltpu.PrefetchScalarGridSpec(
            num_scalar_prefetch=1,
            grid=(samples // (HALVES * lanes),),
            in_specs=[
                pl.BlockSpec((bag, HALVES * lanes), lambda i, h: (0, i)),
                pl.BlockSpec((1, HALVES * lanes), lambda i, h: (0, i)),
            ],
            out_specs=[
                pl.BlockSpec((HALVES, rows, lanes), lambda i, h: (0, 0, i)),
                pl.BlockSpec((8, 128), lambda i, h: (0, 0)),
            ],
        ),
        out_shape=[
            jax.ShapeDtypeStruct((HALVES, rows, samples // HALVES), BF16),
            jax.ShapeDtypeStruct((8, 128), F32),
        ],
        compiler_params=LIMIT,
        cost_estimate=pl.CostEstimate(
            flops=3 * bag * rows * samples, bytes_accessed=2 * rows * samples, transcendentals=0
        ),
    )(half, index_cols, bag_lengths)


def products(cot, feats, weights):
    wgrad = lax.dot_general(feats, cot, (((0,), (0,)), ((), ())), preferred_element_type=F32)
    pgrad = lax.dot_general(cot, weights, (((1,), (1,)), ((), ())), preferred_element_type=F32)
    return wgrad, pgrad.astype(BF16)


def partner_kernel(cot_ref, feats_ref, weight_ref, counted_ref, o_ref, total_ref):
    del counted_ref
    k = pl.program_id(0)
    cot = cot_ref[0]
    emb, width = total_ref.shape
    weights = along(weight_ref[0].reshape(width, emb), emb)
    wgrad, pgrad = products(cot, feats_ref[...].reshape(cot.shape[0], emb), weights)
    ring, own = o_ref.shape[1], o_ref.shape[3]
    o_ref[0, :, k] = pgrad.reshape(ring, own, emb)

    @pl.when(k == 0)
    def _():
        total_ref[...] = wgrad

    @pl.when(k > 0)
    def _():
        total_ref[...] += wgrad

    @pl.when(k == pl.num_programs(0) - 1)
    def _():
        o_ref[1] = across(total_ref[...].astype(BF16)).reshape(o_ref.shape[1:])


def partner_part(gathered, received, counted):
    sides, rows, width = gathered.shape
    _, ring, _, own, emb = received.shape
    return pl.pallas_call(
        partner_kernel,
        grid=(sides,),
        in_specs=[
            pl.BlockSpec((1, rows, width), lambda k: (k, 0, 0)),
            pl.BlockSpec((1, ring, 1, own, emb), lambda k: (0, 0, k, 0, 0)),
            pl.BlockSpec((1, ring, sides, own, emb), lambda k: (1, 0, 0, 0, 0)),
            pl.BlockSpec(memory_space=pl.ANY),
        ],
        out_specs=pl.BlockSpec(received.shape, lambda k: (0, 0, 0, 0, 0)),
        out_shape=jax.ShapeDtypeStruct(received.shape, BF16),
        scratch_shapes=[pltpu.VMEM((emb, width), F32)],
        compiler_params=LIMIT,
        cost_estimate=pl.CostEstimate(
            flops=4 * sides * rows * emb * width,
            bytes_accessed=2 * sides * rows * width + 4 * received.size,
            transcendentals=0,
        ),
    )(gathered, received, received, counted)


def own_kernel(
    half_ref, cot_ref, feats_ref, weight_ref, counts_ref, wgrad_ref, row_ref, pgrad_ref
):
    k = pl.program_id(0)
    cot = cot_ref[0]
    emb = weight_ref.shape[0]
    ring, sides, own, _ = pgrad_ref.shape
    wgrad, pgrad = products(cot, feats_ref[...].reshape(cot.shape[0], emb), weight_ref[...])
    pgrad_ref[:, k] = pgrad.reshape(ring, own, emb)

    @pl.when(k == 0)
    def _():
        wgrad_ref[...] = wgrad

    @pl.when(k > 0)
    def _():
        wgrad_ref[...] += wgrad

    @pl.when(k == pl.num_programs(0) - 1)
    def _():
        row_ref[...] = jnp.dot(
            counts_ref[0],
            pgrad_ref[...].reshape(ring * sides * own, emb),
            preferred_element_type=F32,
        )


def own_part(half, gathered, feats, weights, counts):
    sides, rows, width = gathered.shape
    ring, _, _, own, emb = feats.shape
    _, table_rows, samples = counts.shape
    return pl.pallas_call(
        own_kernel,
        grid_spec=pltpu.PrefetchScalarGridSpec(
            num_scalar_prefetch=1,
            grid=(sides,),
            in_specs=[
                pl.BlockSpec((1, rows, width), lambda k, h: (k, 0, 0)),
                pl.BlockSpec((ring, 1, 1, own, emb), lambda k, h: (0, h[0], k, 0, 0)),
                pl.BlockSpec((emb, width), lambda k, h: (0, 0)),
                pl.BlockSpec((1, table_rows, samples), lambda k, h: (0, 0, 0)),
            ],
            out_specs=[
                pl.BlockSpec((emb, width), lambda k, h: (0, 0)),
                pl.BlockSpec((table_rows, emb), lambda k, h: (0, 0)),
            ],
            scratch_shapes=[pltpu.VMEM((ring, sides, own, emb), BF16)],
        ),
        out_shape=[
            jax.ShapeDtypeStruct((emb, width), F32),
            jax.ShapeDtypeStruct((table_rows, emb), F32),
        ],
        compiler_params=LIMIT,
        cost_estimate=pl.CostEstimate(
            flops=4 * sides * rows * emb * width + 2 * samples * emb * table_rows,
            bytes_accessed=2 * sides * rows * width + 8 * emb * width,
            transcendentals=0,
        ),
    )(half, gathered, feats, weights, counts)


def update_kernel(
    other_ref, share_ref, row_ref, counts_ref, slab_ref, sums_ref,
    wgrad_ref, table_ref, fresh_ref,
):
    _, ring, sides, own, emb = other_ref.shape

    @pl.when(pl.program_id(0) == 0)
    def _():
        width = share_ref.shape[1]
        wgrad_ref[...] = share_ref[...] + along(other_ref[1].reshape(width, emb), emb).astype(F32)

    row_grad = row_ref[...] + jnp.dot(
        counts_ref[0],
        other_ref[0].reshape(ring * sides * own, emb),
        preferred_element_type=F32,
    )
    fresh = sums_ref[...] + row_grad * row_grad
    fresh_ref[...] = fresh
    table_ref[...] = slab_ref[...] - learn_rate * row_grad / (jnp.sqrt(fresh) + epsilon)


def update(other, share, row_share, counts, slab, sums):
    _, rows, samples = counts.shape
    emb, width = share.shape
    steps = 4
    tile = rows // steps
    return pl.pallas_call(
        update_kernel,
        grid=(steps,),
        in_specs=[
            pl.BlockSpec(other.shape, lambda k: (0, 0, 0, 0, 0)),
            pl.BlockSpec((emb, width), lambda k: (0, 0)),
            pl.BlockSpec((tile, emb), lambda k: (k, 0)),
            pl.BlockSpec((1, tile, samples), lambda k: (1, k, 0)),
            pl.BlockSpec((tile, emb), lambda k: (k, 0)),
            pl.BlockSpec((tile, emb), lambda k: (k, 0)),
        ],
        out_specs=[
            pl.BlockSpec((emb, width), lambda k: (0, 0)),
            pl.BlockSpec((tile, emb), lambda k: (k, 0)),
            pl.BlockSpec((tile, emb), lambda k: (k, 0)),
        ],
        out_shape=[
            jax.ShapeDtypeStruct((emb, width), F32),
            jax.ShapeDtypeStruct((rows, emb), F32),
            jax.ShapeDtypeStruct((rows, emb), F32),
        ],
        compiler_params=LIMIT,
        cost_estimate=pl.CostEstimate(
            flops=2 * samples * emb * rows,
            bytes_accessed=2 * samples * rows + 16 * rows * emb + 12 * emb * width,
            transcendentals=rows * emb,
        ),
    )(other, share, row_share, counts, slab, sums)


def per_device(grad_inter, pooled, tower_weight, indices, lengths, table_slab, accumulator):
    towers, ring_size, sides = (lax.axis_size(a) for a in ("tower", RING, SIDE))
    pairs = partners(towers, ring_size * HALVES)
    half = lax.axis_index(HALF).astype(jnp.int32).reshape(1)
    weights = tower_weight[0]
    feats = pooled[0].reshape(ring_size, HALVES, sides, -1, pooled.shape[2])

    parted, to_partner = prepare(half, grad_inter[0], towers, feats, weights)
    from_partner = lax.ppermute(to_partner, PAIRED, pairs)
    own = lax.all_to_all(parted, "tower", split_axis=0, concat_axis=0)
    own = own.reshape(-1, own.shape[2])
    ring = lax.all_gather(own, RING, axis=0, tiled=True)
    gathered = lax.all_to_all(
        jnp.broadcast_to(ring[None], (sides,) + ring.shape), SIDE, split_axis=0, concat_axis=0
    )
    counts, counted = bag_counts(half, indices[0, 0].T, lengths[0], table_slab.shape[1])

    other = lax.ppermute(partner_part(gathered, from_partner, counted), PAIRED, pairs)
    share, row_share = own_part(half, gathered, feats, weights, counts)
    wgrad, updated, fresh = update(
        other, share, row_share, counts, table_slab[0], accumulator[0]
    )
    return (wgrad[None], updated[None], fresh[None])


def solution(mesh):
    towers, inner = mesh.devices.shape
    ring_size, sides = 16, 4
    fine = Mesh(
        mesh.devices.reshape(towers, ring_size, HALVES, sides), ("tower",) + INNER
    )
    return jax.shard_map(
        per_device,
        mesh=fine,
        in_specs=(
            P(INNER, "tower", None),
            P("tower", None, INNER),
            P("tower", INNER, None),
            P("tower", INNER, None, None),
            P("tower", INNER, None),
            P("tower", INNER, None),
            P("tower", INNER, None),
        ),
        out_specs=(P("tower", INNER, None), P("tower", INNER, None), P("tower", INNER, None)),
        check_vma=False,
    )
```

```python
import functools

import jax
import jax.numpy as jnp
from jax import lax
from jax.experimental import pallas as pl
from jax.experimental.pallas import tpu as pltpu
from jax.sharding import Mesh, PartitionSpec as P

learn_rate = 0.1
epsilon = 1e-08

HALVES = 2
RING, HALF, SIDE = "ring", "half", "side"
INNER = (RING, HALF, SIDE)
PAIRED = ("tower", RING, HALF)

BF16 = jnp.bfloat16
F32 = jnp.float32
LIMIT = pltpu.CompilerParams(vmem_limit_bytes=20 * 1024 * 1024)


def partners(towers, length):
    pairs = []
    for t in range(towers):
        for z in range(length):
            up = (z + t) % 2 == 0
            pairs.append((t * length + z, t * length + (z + (1 if up else -1)) % length))
    return pairs


def across(w):
    rows, cols = w.shape
    return jnp.concatenate([w[:, i:i + rows] for i in range(0, cols, rows)], axis=0)


def along(w, rows):
    return jnp.concatenate([w[i:i + rows] for i in range(0, w.shape[0], rows)], axis=1)


def split_kernel(x_ref, o_ref):
    towers, _, width = o_ref.shape
    for t in range(towers):
        o_ref[t] = x_ref[:, t * width:(t + 1) * width]


def split_towers(x, towers):
    rows, width = x.shape
    return pl.pallas_call(
        split_kernel,
        out_shape=pltpu.VMEM((towers, rows, width // towers), x.dtype),
    )(x)


def copies_kernel(x_ref, o_ref, sems):
    copies = [
        pltpu.make_async_copy(x_ref, o_ref.at[i], sems.at[i]) for i in range(o_ref.shape[0])
    ]
    for copy in copies:
        copy.start()
    for copy in copies:
        copy.wait()


def copies_of(x, times):
    return pl.pallas_call(
        copies_kernel,
        in_specs=[pl.BlockSpec(memory_space=pltpu.VMEM)],
        out_specs=pl.BlockSpec(memory_space=pl.ANY),
        out_shape=pltpu.HBM((times,) + x.shape, x.dtype),
        scratch_shapes=[pltpu.SemaphoreType.DMA((times,))],
        compiler_params=LIMIT,
    )(pltpu.with_memory_space_constraint(x, pltpu.VMEM))


def prepare_kernel(half_ref, pooled_ref, weight_ref, send_ref):
    send_ref[0] = pooled_ref[:, 0]
    send_ref[1] = across(weight_ref[...]).reshape(send_ref.shape[1:])


def prepare(half, feats, weights):
    ring, halves, sides, own, emb = feats.shape
    return pl.pallas_call(
        prepare_kernel,
        grid_spec=pltpu.PrefetchScalarGridSpec(
            num_scalar_prefetch=1,
            grid=(1,),
            in_specs=[
                pl.BlockSpec((ring, 1, sides, own, emb), lambda k, h: (0, 1 - h[0], 0, 0, 0)),
                pl.BlockSpec(weights.shape, lambda k, h: (0, 0)),
            ],
            out_specs=pl.BlockSpec((2, ring, sides, own, emb), lambda k, h: (0, 0, 0, 0, 0)),
        ),
        out_shape=jax.ShapeDtypeStruct((2, ring, sides, own, emb), BF16),
        compiler_params=LIMIT,
    )(half, feats, weights)


def count_kernel(half_ref, index_ref, length_ref, o_ref, done_ref):
    done_ref[...] = jnp.zeros_like(done_ref)
    bag, width = index_ref.shape
    _, rows, lanes = o_ref.shape
    step = 16
    run = lanes // 2
    bag_at = lax.broadcasted_iota(jnp.int32, index_ref.shape, 0)
    live = jnp.where(bag_at < length_ref[...], index_ref[...], -1)
    left, right = live[:, :lanes], live[:, lanes:]
    low_lane = lax.broadcasted_iota(jnp.int32, left.shape, 1) < run
    halves = [
        jnp.where(low_lane, left, pltpu.roll(right, run, 1)),
        jnp.where(low_lane, pltpu.roll(left, run, 1), right),
    ]
    upper = half_ref[0] == 1
    first = lax.broadcasted_iota(jnp.int32, (step, lanes), 0)
    for side in range(2):
        chosen = jnp.where(upper, halves[1 - side], halves[side])
        entries = [
            jnp.broadcast_to(chosen[b:b + 1, :], (step, lanes)).astype(jnp.int16)
            for b in range(bag)
        ]

        def body(k, _, entries=entries, side=side):
            low = pl.multiple_of(k * step, step)
            row = (first + low).astype(jnp.int16)
            parts = [jnp.where(e == row, jnp.ones((), BF16), jnp.zeros((), BF16)) for e in entries]
            while len(parts) > 1:
                parts = [parts[i] + parts[i + 1] for i in range(0, len(parts), 2)]
            o_ref[side, pl.ds(low, step), :] = parts[0]
            return 0

        lax.fori_loop(0, rows // step, body, 0, unroll=4)


def bag_counts(half, index_cols, bag_lengths, rows):
    bag, samples = index_cols.shape
    lanes = 128
    return pl.pallas_call(
        count_kernel,
        grid_spec=pltpu.PrefetchScalarGridSpec(
            num_scalar_prefetch=1,
            grid=(samples // (HALVES * lanes),),
            in_specs=[
                pl.BlockSpec((bag, HALVES * lanes), lambda i, h: (0, i)),
                pl.BlockSpec((1, HALVES * lanes), lambda i, h: (0, i)),
            ],
            out_specs=[
                pl.BlockSpec((HALVES, rows, lanes), lambda i, h: (0, 0, i)),
                pl.BlockSpec((8, 128), lambda i, h: (0, 0)),
            ],
        ),
        out_shape=[
            pltpu.HBM((HALVES, rows, samples // HALVES), BF16),
            jax.ShapeDtypeStruct((8, 128), F32),
        ],
        compiler_params=LIMIT,
        cost_estimate=pl.CostEstimate(
            flops=3 * bag * rows * samples, bytes_accessed=2 * rows * samples, transcendentals=0
        ),
    )(half, index_cols, bag_lengths)


def products(cot, feats, weights):
    wgrad = lax.dot_general(feats, cot, (((0,), (0,)), ((), ())), preferred_element_type=F32)
    pgrad = lax.dot_general(cot, weights, (((1,), (1,)), ((), ())), preferred_element_type=F32)
    return wgrad, pgrad.astype(BF16)


def partner_kernel(cot_ref, feats_ref, weight_ref, counted_ref, o_ref, total_ref):
    del counted_ref
    k = pl.program_id(0)
    emb, width = total_ref.shape
    weights = along(weight_ref[0].reshape(width, emb), emb)
    ring, own = o_ref.shape[1], o_ref.shape[3]
    blocks, rows, _ = cot_ref.shape
    wgrad = jnp.zeros((emb, width), F32)
    for i in range(blocks):
        share, pgrad = products(cot_ref[i], feats_ref[0, :, i].reshape(rows, emb), weights)
        o_ref[0, :, k * blocks + i] = pgrad.reshape(ring, own, emb)
        wgrad += share

    @pl.when(k == 0)
    def _():
        total_ref[...] = wgrad

    @pl.when(k > 0)
    def _():
        total_ref[...] += wgrad

    @pl.when(k == pl.num_programs(0) - 1)
    def _():
        o_ref[1] = across(total_ref[...].astype(BF16)).reshape(o_ref.shape[1:])


def partner_part(gathered, received, counted):
    sides, rows, width = gathered.shape
    _, ring, _, own, emb = received.shape
    steps = 2
    blocks = sides // steps
    return pl.pallas_call(
        partner_kernel,
        grid=(steps,),
        in_specs=[
            pl.BlockSpec((blocks, rows, width), lambda k: (k, 0, 0)),
            pl.BlockSpec((1, ring, blocks, own, emb), lambda k: (0, 0, k, 0, 0)),
            pl.BlockSpec((1, ring, sides, own, emb), lambda k: (1, 0, 0, 0, 0)),
            pl.BlockSpec(memory_space=pl.ANY),
        ],
        out_specs=pl.BlockSpec(received.shape, lambda k: (0, 0, 0, 0, 0)),
        out_shape=jax.ShapeDtypeStruct(received.shape, BF16),
        scratch_shapes=[pltpu.VMEM((emb, width), F32)],
        compiler_params=LIMIT,
        cost_estimate=pl.CostEstimate(
            flops=4 * sides * rows * emb * width,
            bytes_accessed=2 * sides * rows * width + 4 * received.size,
            transcendentals=0,
        ),
    )(gathered, received, received, counted)


def own_kernel(
    half_ref, cot_ref, feats_ref, weight_ref, counts_ref, wgrad_ref, row_ref, pgrad_ref
):
    k = pl.program_id(0)
    cot = cot_ref[0]
    emb = weight_ref.shape[0]
    ring, sides, own, _ = pgrad_ref.shape
    wgrad, pgrad = products(cot, feats_ref[...].reshape(cot.shape[0], emb), weight_ref[...])
    pgrad_ref[:, k] = pgrad.reshape(ring, own, emb)

    @pl.when(k == 0)
    def _():
        wgrad_ref[...] = wgrad

    @pl.when(k > 0)
    def _():
        wgrad_ref[...] += wgrad

    @pl.when(k == pl.num_programs(0) - 1)
    def _():
        row_ref[...] = jnp.dot(
            counts_ref[0],
            pgrad_ref[...].reshape(ring * sides * own, emb),
            preferred_element_type=F32,
        )


def own_part(half, gathered, feats, weights, counts):
    sides, rows, width = gathered.shape
    ring, _, _, own, emb = feats.shape
    _, table_rows, samples = counts.shape
    return pl.pallas_call(
        own_kernel,
        grid_spec=pltpu.PrefetchScalarGridSpec(
            num_scalar_prefetch=1,
            grid=(sides,),
            in_specs=[
                pl.BlockSpec((1, rows, width), lambda k, h: (k, 0, 0)),
                pl.BlockSpec((ring, 1, 1, own, emb), lambda k, h: (0, h[0], k, 0, 0)),
                pl.BlockSpec((emb, width), lambda k, h: (0, 0)),
                pl.BlockSpec((1, table_rows, samples), lambda k, h: (0, 0, 0)),
            ],
            out_specs=[
                pl.BlockSpec((emb, width), lambda k, h: (0, 0)),
                pl.BlockSpec((table_rows, emb), lambda k, h: (0, 0)),
            ],
            scratch_shapes=[pltpu.VMEM((ring, sides, own, emb), BF16)],
        ),
        out_shape=[
            jax.ShapeDtypeStruct((emb, width), F32),
            jax.ShapeDtypeStruct((table_rows, emb), F32),
        ],
        compiler_params=LIMIT,
        cost_estimate=pl.CostEstimate(
            flops=4 * sides * rows * emb * width + 2 * samples * emb * table_rows,
            bytes_accessed=2 * sides * rows * width + 8 * emb * width,
            transcendentals=0,
        ),
    )(half, gathered, feats, weights, counts)


def update_kernel(
    other_ref, part_ref, share_ref, row_ref, counts_ref, slab_ref, sums_ref,
    wgrad_ref, table_ref, fresh_ref,
):
    _, ring, sides, own, emb = other_ref.shape
    width = share_ref.shape[1]
    part = part_ref[0].reshape(width, emb)
    wgrad_ref[...] = share_ref[...] + along(part, emb).astype(F32)

    row_grad = row_ref[...] + jnp.dot(
        counts_ref[0],
        other_ref[0].reshape(ring * sides * own, emb),
        preferred_element_type=F32,
    )
    fresh = sums_ref[...] + row_grad * row_grad
    fresh_ref[...] = fresh
    table_ref[...] = slab_ref[...] - learn_rate * row_grad / (jnp.sqrt(fresh) + epsilon)


def update(other, share, row_share, counts, slab, sums):
    _, rows, samples = counts.shape
    emb, width = share.shape
    steps = 2
    tile = rows // steps
    return pl.pallas_call(
        update_kernel,
        grid=(steps,),
        in_specs=[
            pl.BlockSpec((1,) + other.shape[1:], lambda k: (0, 0, 0, 0, 0)),
            pl.BlockSpec((1, other.shape[1] // steps) + other.shape[2:], lambda k: (1, k, 0, 0, 0)),
            pl.BlockSpec((emb, width // steps), lambda k: (0, k)),
            pl.BlockSpec((tile, emb), lambda k: (k, 0)),
            pl.BlockSpec((1, tile, samples), lambda k: (1, k, 0)),
            pl.BlockSpec((tile, emb), lambda k: (k, 0)),
            pl.BlockSpec((tile, emb), lambda k: (k, 0)),
        ],
        out_specs=[
            pl.BlockSpec((emb, width // steps), lambda k: (0, k)),
            pl.BlockSpec((tile, emb), lambda k: (k, 0)),
            pl.BlockSpec((tile, emb), lambda k: (k, 0)),
        ],
        out_shape=[
            jax.ShapeDtypeStruct((emb, width), F32),
            jax.ShapeDtypeStruct((rows, emb), F32),
            jax.ShapeDtypeStruct((rows, emb), F32),
        ],
        compiler_params=LIMIT,
        cost_estimate=pl.CostEstimate(
            flops=2 * samples * emb * rows,
            bytes_accessed=2 * samples * rows + 16 * rows * emb + 12 * emb * width,
            transcendentals=rows * emb,
        ),
    )(other, other, share, row_share, counts, slab, sums)


def per_device(grad_inter, pooled, tower_weight, indices, lengths, table_slab, accumulator):
    towers, ring_size, sides = (lax.axis_size(a) for a in ("tower", RING, SIDE))
    pairs = partners(towers, ring_size * HALVES)
    half = lax.axis_index(HALF).astype(jnp.int32).reshape(1)
    weights = tower_weight[0]
    feats = pooled[0].reshape(ring_size, HALVES, sides, -1, pooled.shape[2])

    from_partner = lax.ppermute(prepare(half, feats, weights), PAIRED, pairs)
    own = lax.all_to_all(split_towers(grad_inter[0], towers), "tower", split_axis=0, concat_axis=0)
    own = own.reshape(-1, own.shape[2])
    ring = lax.all_gather(own, RING, axis=0, tiled=True)
    gathered = lax.all_to_all(copies_of(ring, sides), SIDE, split_axis=0, concat_axis=0)
    counts, counted = bag_counts(half, indices[0, 0].T, lengths[0], table_slab.shape[1])

    other = lax.ppermute(partner_part(gathered, from_partner, counted), PAIRED, pairs)
    share, row_share = own_part(half, gathered, feats, weights, counts)
    wgrad, updated, fresh = update(
        other, share, row_share, counts, table_slab[0], accumulator[0]
    )
    return (wgrad[None], updated[None], fresh[None])


def solution(mesh):
    towers, inner = mesh.devices.shape
    ring_size, sides = 16, 4
    fine = Mesh(
        mesh.devices.reshape(towers, ring_size, HALVES, sides), ("tower",) + INNER
    )
    return jax.shard_map(
        per_device,
        mesh=fine,
        in_specs=(
            P(INNER, "tower", None),
            P("tower", None, INNER),
            P("tower", INNER, None),
            P("tower", INNER, None, None),
            P("tower", INNER, None),
            P("tower", INNER, None),
            P("tower", INNER, None),
        ),
        out_specs=(P("tower", INNER, None), P("tower", INNER, None), P("tower", INNER, None)),
        check_vma=False,
    )
```

```python
import functools

import jax
import jax.numpy as jnp
from jax import lax
from jax.experimental import pallas as pl
from jax.experimental.pallas import tpu as pltpu
from jax.sharding import Mesh, PartitionSpec as P

learn_rate = 0.1
epsilon = 1e-08

HALVES = 2
RING, HALF, SIDE = "ring", "half", "side"
INNER = (RING, HALF, SIDE)
PAIRED = ("tower", RING, HALF)

BF16 = jnp.bfloat16
F32 = jnp.float32
LIMIT = pltpu.CompilerParams(vmem_limit_bytes=20 * 1024 * 1024)


def partners(towers, length):
    pairs = []
    for t in range(towers):
        for z in range(length):
            up = (z + t) % 2 == 0
            pairs.append((t * length + z, t * length + (z + (1 if up else -1)) % length))
    return pairs


def across(w):
    rows, cols = w.shape
    return jnp.concatenate([w[:, i:i + rows] for i in range(0, cols, rows)], axis=0)


def along(w, rows):
    return jnp.concatenate([w[i:i + rows] for i in range(0, w.shape[0], rows)], axis=1)


def split_kernel(x_ref, o_ref):
    towers, _, width = o_ref.shape
    for t in range(towers):
        o_ref[t] = x_ref[:, t * width:(t + 1) * width]


def split_towers(x, towers):
    rows, width = x.shape
    return pl.pallas_call(
        split_kernel,
        out_shape=pltpu.VMEM((towers, rows, width // towers), x.dtype),
    )(x)


def copies_kernel(x_ref, o_ref, sems):
    copies = [
        pltpu.make_async_copy(x_ref, o_ref.at[i], sems.at[i]) for i in range(o_ref.shape[0])
    ]
    for copy in copies:
        copy.start()
    for copy in copies:
        copy.wait()


def copies_of(x, times):
    return pl.pallas_call(
        copies_kernel,
        in_specs=[pl.BlockSpec(memory_space=pltpu.VMEM)],
        out_specs=pl.BlockSpec(memory_space=pl.ANY),
        out_shape=pltpu.HBM((times,) + x.shape, x.dtype),
        scratch_shapes=[pltpu.SemaphoreType.DMA((times,))],
        compiler_params=LIMIT,
    )(pltpu.with_memory_space_constraint(x, pltpu.VMEM))


def prepare_kernel(half_ref, pooled_ref, weight_ref, send_ref):
    send_ref[0] = pooled_ref[:, 0]
    send_ref[1] = across(weight_ref[...]).reshape(send_ref.shape[1:])


def prepare(half, feats, weights):
    ring, halves, sides, own, emb = feats.shape
    return pl.pallas_call(
        prepare_kernel,
        grid_spec=pltpu.PrefetchScalarGridSpec(
            num_scalar_prefetch=1,
            grid=(1,),
            in_specs=[
                pl.BlockSpec((ring, 1, sides, own, emb), lambda k, h: (0, 1 - h[0], 0, 0, 0)),
                pl.BlockSpec(weights.shape, lambda k, h: (0, 0)),
            ],
            out_specs=pl.BlockSpec((2, ring, sides, own, emb), lambda k, h: (0, 0, 0, 0, 0)),
        ),
        out_shape=jax.ShapeDtypeStruct((2, ring, sides, own, emb), BF16),
        compiler_params=LIMIT,
    )(half, feats, weights)


def count_kernel(half_ref, index_ref, length_ref, o_ref, done_ref):
    done_ref[...] = jnp.zeros_like(done_ref)
    bag, width = index_ref.shape
    _, rows, lanes = o_ref.shape
    step = 16
    run = lanes // 2
    bag_at = lax.broadcasted_iota(jnp.int32, index_ref.shape, 0)
    live = jnp.where(bag_at < length_ref[...], index_ref[...], -1)
    left, right = live[:, :lanes], live[:, lanes:]
    low_lane = lax.broadcasted_iota(jnp.int32, left.shape, 1) < run
    halves = [
        jnp.where(low_lane, left, pltpu.roll(right, run, 1)),
        jnp.where(low_lane, pltpu.roll(left, run, 1), right),
    ]
    upper = half_ref[0] == 1
    first = lax.broadcasted_iota(jnp.int32, (step, lanes), 0)
    for side in range(2):
        chosen = jnp.where(upper, halves[1 - side], halves[side])
        entries = [
            jnp.broadcast_to(chosen[b:b + 1, :], (step, lanes)).astype(jnp.int16)
            for b in range(bag)
        ]

        def body(k, _, entries=entries, side=side):
            low = pl.multiple_of(k * step, step)
            row = (first + low).astype(jnp.int16)
            parts = [jnp.where(e == row, jnp.ones((), BF16), jnp.zeros((), BF16)) for e in entries]
            while len(parts) > 1:
                parts = [parts[i] + parts[i + 1] for i in range(0, len(parts), 2)]
            o_ref[side, pl.ds(low, step), :] = parts[0]
            return 0

        lax.fori_loop(0, rows // step, body, 0, unroll=4)


def bag_counts(half, index_cols, bag_lengths, rows):
    bag, samples = index_cols.shape
    lanes = 128
    return pl.pallas_call(
        count_kernel,
        grid_spec=pltpu.PrefetchScalarGridSpec(
            num_scalar_prefetch=1,
            grid=(samples // (HALVES * lanes),),
            in_specs=[
                pl.BlockSpec((bag, HALVES * lanes), lambda i, h: (0, i)),
                pl.BlockSpec((1, HALVES * lanes), lambda i, h: (0, i)),
            ],
            out_specs=[
                pl.BlockSpec((HALVES, rows, lanes), lambda i, h: (0, 0, i)),
                pl.BlockSpec((8, 128), lambda i, h: (0, 0)),
            ],
        ),
        out_shape=[
            pltpu.HBM((HALVES, rows, samples // HALVES), BF16),
            jax.ShapeDtypeStruct((8, 128), F32),
        ],
        compiler_params=LIMIT,
        cost_estimate=pl.CostEstimate(
            flops=3 * bag * rows * samples, bytes_accessed=2 * rows * samples, transcendentals=0
        ),
    )(half, index_cols, bag_lengths)


def products(cot, feats, weights):
    wgrad = lax.dot_general(feats, cot, (((0,), (0,)), ((), ())), preferred_element_type=F32)
    pgrad = lax.dot_general(cot, weights, (((1,), (1,)), ((), ())), preferred_element_type=F32)
    return wgrad, pgrad.astype(BF16)


def partner_kernel(cot_ref, received_ref, counted_ref, o_ref):
    del counted_ref
    _, ring, sides, own, emb = o_ref.shape
    _, rows, width = cot_ref.shape
    weights = along(received_ref[1].reshape(width, emb), emb)
    wgrad = jnp.zeros((emb, width), F32)
    for k in range(sides):
        share, pgrad = products(cot_ref[k], received_ref[0, :, k].reshape(rows, emb), weights)
        o_ref[0, :, k] = pgrad.reshape(ring, own, emb)
        wgrad += share
    o_ref[1] = across(wgrad.astype(BF16)).reshape(o_ref.shape[1:])


def partner_part(gathered, received, counted):
    sides, rows, width = gathered.shape
    emb = received.shape[-1]
    return pl.pallas_call(
        partner_kernel,
        in_specs=[
            pl.BlockSpec(memory_space=pltpu.VMEM),
            pl.BlockSpec(memory_space=pltpu.VMEM),
            pl.BlockSpec(memory_space=pl.ANY),
        ],
        out_specs=pl.BlockSpec(memory_space=pltpu.VMEM),
        out_shape=jax.ShapeDtypeStruct(received.shape, BF16),
        compiler_params=LIMIT,
        cost_estimate=pl.CostEstimate(
            flops=4 * sides * rows * emb * width,
            bytes_accessed=2 * sides * rows * width + 4 * received.size,
            transcendentals=0,
        ),
    )(
        pltpu.with_memory_space_constraint(gathered, pltpu.VMEM),
        pltpu.with_memory_space_constraint(received, pltpu.VMEM),
        counted,
    )


def own_kernel(
    half_ref, cot_ref, feats_ref, weight_ref, counts_ref, wgrad_ref, row_ref, pgrad_ref
):
    k = pl.program_id(0)
    cot = cot_ref[0]
    emb = weight_ref.shape[0]
    ring, sides, own, _ = pgrad_ref.shape
    wgrad, pgrad = products(cot, feats_ref[...].reshape(cot.shape[0], emb), weight_ref[...])
    pgrad_ref[:, k] = pgrad.reshape(ring, own, emb)

    @pl.when(k == 0)
    def _():
        wgrad_ref[...] = wgrad

    @pl.when(k > 0)
    def _():
        wgrad_ref[...] += wgrad

    @pl.when(k == pl.num_programs(0) - 1)
    def _():
        row_ref[...] = jnp.dot(
            counts_ref[0],
            pgrad_ref[...].reshape(ring * sides * own, emb),
            preferred_element_type=F32,
        )


def own_part(half, gathered, feats, weights, counts):
    sides, rows, width = gathered.shape
    ring, _, _, own, emb = feats.shape
    _, table_rows, samples = counts.shape
    return pl.pallas_call(
        own_kernel,
        grid_spec=pltpu.PrefetchScalarGridSpec(
            num_scalar_prefetch=1,
            grid=(sides,),
            in_specs=[
                pl.BlockSpec((1, rows, width), lambda k, h: (k, 0, 0)),
                pl.BlockSpec((ring, 1, 1, own, emb), lambda k, h: (0, h[0], k, 0, 0)),
                pl.BlockSpec((emb, width), lambda k, h: (0, 0)),
                pl.BlockSpec((1, table_rows, samples), lambda k, h: (0, 0, 0)),
            ],
            out_specs=[
                pl.BlockSpec((emb, width), lambda k, h: (0, 0)),
                pl.BlockSpec((table_rows, emb), lambda k, h: (0, 0)),
            ],
            scratch_shapes=[pltpu.VMEM((ring, sides, own, emb), BF16)],
        ),
        out_shape=[
            jax.ShapeDtypeStruct((emb, width), F32),
            jax.ShapeDtypeStruct((table_rows, emb), F32),
        ],
        compiler_params=LIMIT,
        cost_estimate=pl.CostEstimate(
            flops=4 * sides * rows * emb * width + 2 * samples * emb * table_rows,
            bytes_accessed=2 * sides * rows * width + 8 * emb * width,
            transcendentals=0,
        ),
    )(half, gathered, feats, weights, counts)


def update_kernel(
    other_ref, share_ref, row_ref, counts_ref, slab_ref, sums_ref,
    wgrad_ref, table_ref, fresh_ref,
):
    _, ring, sides, own, emb = other_ref.shape
    step = pl.program_id(0)
    width = wgrad_ref.shape[1]
    tile = table_ref.shape[0]
    tiles = ring * width // share_ref.shape[1]
    part = other_ref[1, pl.ds(step * tiles, tiles)].reshape(width, emb)
    columns = pl.ds(pl.multiple_of(step * width, width), width)
    wgrad_ref[...] = share_ref[:, columns] + along(part, emb).astype(F32)
    rows = pl.ds(pl.multiple_of(step * tile, tile), tile)
    row_grad = row_ref[rows, :] + jnp.dot(
        counts_ref[1, rows, :],
        other_ref[0].reshape(ring * sides * own, emb),
        preferred_element_type=F32,
    )
    fresh = sums_ref[rows, :] + row_grad * row_grad
    fresh_ref[...] = fresh
    table_ref[...] = slab_ref[rows, :] - learn_rate * row_grad / (jnp.sqrt(fresh) + epsilon)


def update(other, share, row_share, counts, slab, sums):
    _, rows, samples = counts.shape
    emb, width = share.shape
    steps = 2
    tile = rows // steps
    near = [
        pltpu.with_memory_space_constraint(x, pltpu.VMEM)
        for x in (other, share, row_share, counts, slab, sums)
    ]
    return pl.pallas_call(
        update_kernel,
        grid=(steps,),
        in_specs=[pl.BlockSpec(memory_space=pltpu.VMEM)] * len(near),
        out_specs=[
            pl.BlockSpec((emb, width // steps), lambda k: (0, k)),
            pl.BlockSpec((tile, emb), lambda k: (k, 0)),
            pl.BlockSpec((tile, emb), lambda k: (k, 0)),
        ],
        out_shape=[
            jax.ShapeDtypeStruct((emb, width), F32),
            jax.ShapeDtypeStruct((rows, emb), F32),
            jax.ShapeDtypeStruct((rows, emb), F32),
        ],
        compiler_params=LIMIT,
        cost_estimate=pl.CostEstimate(
            flops=2 * samples * emb * rows,
            bytes_accessed=2 * samples * rows + 16 * rows * emb + 12 * emb * width,
            transcendentals=rows * emb,
        ),
    )(*near)


def per_device(grad_inter, pooled, tower_weight, indices, lengths, table_slab, accumulator):
    towers, ring_size, sides = (lax.axis_size(a) for a in ("tower", RING, SIDE))
    pairs = partners(towers, ring_size * HALVES)
    half = lax.axis_index(HALF).astype(jnp.int32).reshape(1)
    weights = tower_weight[0]
    feats = pooled[0].reshape(ring_size, HALVES, sides, -1, pooled.shape[2])

    from_partner = lax.ppermute(prepare(half, feats, weights), PAIRED, pairs)
    own = lax.all_to_all(split_towers(grad_inter[0], towers), "tower", split_axis=0, concat_axis=0)
    own = own.reshape(-1, own.shape[2])
    ring = lax.all_gather(own, RING, axis=0, tiled=True)
    gathered = lax.all_to_all(copies_of(ring, sides), SIDE, split_axis=0, concat_axis=0)
    counts, counted = bag_counts(half, indices[0, 0].T, lengths[0], table_slab.shape[1])

    other = lax.ppermute(partner_part(gathered, from_partner, counted), PAIRED, pairs)
    share, row_share = own_part(half, gathered, feats, weights, counts)
    wgrad, updated, fresh = update(
        other, share, row_share, counts, table_slab[0], accumulator[0]
    )
    return (wgrad[None], updated[None], fresh[None])


def solution(mesh):
    towers, inner = mesh.devices.shape
    ring_size, sides = 16, 4
    fine = Mesh(
        mesh.devices.reshape(towers, ring_size, HALVES, sides), ("tower",) + INNER
    )
    return jax.shard_map(
        per_device,
        mesh=fine,
        in_specs=(
            P(INNER, "tower", None),
            P("tower", None, INNER),
            P("tower", INNER, None),
            P("tower", INNER, None, None),
            P("tower", INNER, None),
            P("tower", INNER, None),
            P("tower", INNER, None),
        ),
        out_specs=(P("tower", INNER, None), P("tower", INNER, None), P("tower", INNER, None)),
        check_vma=False,
    )
```
